32 devices in a mesh: ctx: 8 (over z, y), tp: 4 (over x, core).
Axes of the slice: x: 2, y: 2, z: 4, core: 2. Of those that a mesh axis runs over, the one named last changes fastest.
Arguments:
- stream_in: bfloat16 [8192, 4096], P('ctx', 'tp'), may hold values from -12 to 12
- features: bfloat16 [8192, 3, 4096], P('ctx', None, 'tp'), may hold values from -6 to 6
- mr_taps: float32 [3, 4096, 7], P(None, 'tp'), may hold values from -2 to 2
- mr_filter: bfloat16 [4096, 128], P('tp'), may hold values from -0.5 to 0.5
- norm_gain: float32 [4096], P('tp'), may hold values from 0.1 to 1.9
- li_taps: float32 [3, 4096, 7], P(None, 'tp'), may hold values from -2 to 2
- modal_rates: float32 [4096, 16], P('tp'), may hold values from 2.4414062e-06 to 0.1
- modal_weights: float32 [4096, 16], P('tp'), may hold values from -1.5 to 1.5
Outputs:
- mixed: bfloat16 [8192, 4096], P('ctx', 'tp')
The draws below stay inside these ranges and needn't reach their ends.
All inputs are finite; a program needn't handle non-finite values.
Results may differ from the reference program's by a relative error of at most 0.015.
Values may be sent and summed in bfloat16 or wider, within the bound.
A program may use at most 256 MiB of HBM per device.

```python
import math
import jax
import jax.numpy as jnp
from jax import lax

D = 4096
MODES = 16
SEQ = 8192


def draw_stream_in(key, part):
    first_key, second_key = jax.random.split(key)
    channel_ramp = jnp.arange(D, dtype=jnp.float32) / D
    roughness = jax.random.uniform(second_key, (D,), jnp.float32, 0.7, 1.3)
    scales = jnp.sqrt(1.0 + 2.0 * channel_ramp) * roughness
    values_drawn = jnp.clip(jax.random.normal(first_key, (SEQ, D), jnp.float32), -5.0, 5.0)
    return (values_drawn * scales).astype(jnp.bfloat16)


def shard_levels(own_key, dims, shards, smallest, largest):
    level, own = 1.0, jax.random.fold_in(own_key, 6)
    for axis_at, parts in shards:
        draws = jnp.exp(jax.random.uniform(jax.random.fold_in(own, axis_at), (parts,), jnp.float32, smallest / len(shards), largest / len(shards)))
        level = level * jnp.repeat(draws, dims[axis_at] // parts).reshape([-1 if axis == axis_at else 1 for axis in range(len(dims))])
    return level


def normal_values(own_key, shape, deviation, most, cuts=(), held_as=jnp.bfloat16):
    factor_of = shard_levels(own_key, shape, cuts, -0.22, 0.18) if cuts else 1.0
    values = jax.random.normal(own_key, shape, jnp.float32) * deviation * factor_of
    return jnp.minimum(jnp.maximum(values, -most), most).astype(held_as)


def setup_inputs(seed: int = 0) -> dict:
    key_of = jax.random.split(jax.random.key(seed), 9)
    return {
        "stream_in": draw_stream_in(jax.random.fold_in(key_of[8], 71), 0),
        "features": normal_values(key_of[1], (SEQ, 3, D), 1.0, 6.0, ((0, 8), (2, 4))),
        "mr_taps": normal_values(key_of[2], (3, D, 7), 7 ** -0.5, 2.0, ((1, 4),), jnp.float32),
        "mr_filter": normal_values(key_of[3], (D, 128), 128 ** -0.5, 0.5, ((0, 4),)),
        "norm_gain": jnp.clip(1.0 + 0.18 * jax.random.normal(key_of[4], (D,), jnp.float32), 0.1, 1.9),
        "li_taps": normal_values(key_of[5], (3, D, 7), 7 ** -0.5, 2.0, ((1, 4),), jnp.float32),
        "modal_rates": jnp.clip(jnp.exp(math.log(0.1) - 10.620351 * jax.random.uniform(key_of[6], (D, MODES), jnp.float32) ** shard_levels(key_of[6], (D, MODES), ((0, 4),), -0.2, 0.2)), 2.441406195430318e-06, 0.1),
        "modal_weights": normal_values(key_of[7], (D, MODES), MODES ** -0.5, 1.5, ((0, 4),), jnp.float32),
    }


epsilon = 1e-06
top_precision = lax.Precision.HIGHEST

def short_conv(rows_in, taps, row_count):
    summed = jnp.zeros((row_count, rows_in.shape[1]), jnp.float32)
    for tap_index in range(7):
        summed = summed + taps[:, tap_index] * rows_in[6 - tap_index:6 - tap_index + row_count].astype(jnp.float32)
    return summed

def featurize(rows_in, taps):
    padded = jnp.pad(rows_in, ((6, 0), (0, 0)))
    return short_conv(padded, taps, rows_in.shape[0])

def split_cols(matrix, width):
    return matrix.reshape(matrix.shape[0], -1, width).transpose(1, 0, 2)

def join_cols(pieces):
    return pieces.transpose(1, 0, 2).reshape(pieces.shape[1], -1)

def medium_group(operands):
    product_cols, filt_rows = operands
    group_width = product_cols.shape[1]
    block_count = SEQ // 64
    padded = jnp.pad(product_cols.astype(jnp.float32), ((128, 0), (0, 0))).reshape(block_count + 2, 64, group_width)
    lag_table = jnp.arange(64, dtype=jnp.int32)[:, None] + 128 - jnp.arange(192, dtype=jnp.int32)[None, :]
    valid = (lag_table >= 0) & (lag_table < 128)
    matrix = jnp.where(valid[None], filt_rows.astype(jnp.float32)[:, jnp.clip(lag_table, 0, 127)], 0.0)
    summed = jnp.zeros((block_count, 64, group_width), jnp.float32)
    for part_index in range(3):
        summed = summed + jnp.einsum('cij,bjc->bic', matrix[:, :, 64 * part_index:64 * part_index + 64], padded[part_index:part_index + block_count], precision=top_precision)
    return summed.reshape(SEQ, group_width)

def long_group(operands):
    product_cols, rates, weights = operands
    group_width = product_cols.shape[1]
    block_count = SEQ // 64
    block_groups = product_cols.astype(jnp.float32).reshape(block_count, 64, group_width)
    scaled = weights * jnp.sqrt(1.0 - jnp.exp(-2.0 * rates))
    lags = jnp.arange(64, dtype=jnp.float32)
    near_taps = lax.optimization_barrier(jnp.sum(scaled[:, None, :] * jnp.exp(-rates[:, None, :] * lags[None, :, None]), axis=2))
    lag_table = jnp.arange(64, dtype=jnp.int32)[:, None] - jnp.arange(64, dtype=jnp.int32)[None, :]
    matrix = jnp.where((lag_table >= 0)[None], near_taps[:, jnp.clip(lag_table, 0, 63)], 0.0)
    near = jnp.einsum('cij,bjc->bic', matrix, block_groups, precision=top_precision)
    outgoing_state = jnp.exp(-rates[None] * (63.0 - lags)[:, None, None])
    produced_output = jnp.einsum('bjc,jcn->bcn', block_groups, outgoing_state, precision=top_precision)
    decay = jnp.exp(-rates * 64.0)

    def advance(state, emit):
        return (state * decay + emit, state)
    unused, states = lax.scan(advance, jnp.zeros_like(decay), produced_output)
    incoming_state = scaled[None] * jnp.exp(-rates[None] * (lags + 1.0)[:, None, None])
    distant_taps = jnp.einsum('bcn,icn->bic', states, incoming_state, precision=top_precision)
    return (near + distant_taps).reshape(SEQ, group_width)

def reference(stream_in, features, mr_taps, mr_filter, norm_gain, li_taps, modal_rates, modal_weights):
    group_width = min(256, D)
    gate_one = featurize(features[:, 0], mr_taps[0])
    keys_one = featurize(features[:, 1], mr_taps[1])
    vals_one = featurize(features[:, 2], mr_taps[2])
    product_one = (keys_one * vals_one).astype(jnp.bfloat16)
    medium = join_cols(lax.map(medium_group, (split_cols(product_one, group_width), mr_filter.reshape(-1, group_width, 128))))
    stream = stream_in.astype(jnp.float32) + gate_one * medium
    squares = lax.optimization_barrier(jnp.sum(stream * stream, axis=1)) / D
    normed = (stream * lax.rsqrt(squares + epsilon)[:, None] * norm_gain).astype(jnp.bfloat16)
    gate_two = featurize(normed, li_taps[0])
    keys_two = featurize(normed, li_taps[1])
    vals_two = featurize(normed, li_taps[2])
    product_two = (keys_two * vals_two).astype(jnp.bfloat16)
    long_out = join_cols(lax.map(long_group, (split_cols(product_two, group_width), modal_rates.reshape(-1, group_width, MODES), modal_weights.reshape(-1, group_width, MODES))))
    return (stream + gate_two * long_out).astype(jnp.bfloat16)
```

```python
import functools

import jax
import jax.numpy as jnp
import ml_dtypes
import numpy as np
from jax import lax
from jax.experimental import pallas as pl
from jax.experimental.pallas import tpu as pltpu
from jax.sharding import PartitionSpec as P

EPS = 1e-06
MODES = 16
TAPS = 7
MR = 128
HALO = 144
LEAD = 8
SEGS = 8
NFFT = 512
HALF = NFFT // 2
FIRST = HALO - LEAD
VMEM_LIMIT = 48 * 1024 * 1024
f32 = jnp.float32
bf16 = jnp.bfloat16


def split_np(matrix):
    high = matrix.astype(np.float32).astype(ml_dtypes.bfloat16)
    low = (matrix - high.astype(np.float64)).astype(np.float32).astype(ml_dtypes.bfloat16)
    return high, low


def dft_tables(out_rows):
    k = np.arange(HALF)[:, None]
    i = np.arange(NFFT)[None, :]
    angle = 2.0 * np.pi * ((k * i) % NFFT) / NFFT
    sign = 1.0 - 2.0 * (i % 2)
    forward = np.concatenate([np.cos(angle), -np.sin(angle)], axis=0)
    forward[HALF] = sign[0]
    back = 2.0 * forward.T / NFFT
    back[:, 0] *= 0.5
    back[:, HALF] *= 0.5
    return split_np(forward), split_np(back[FIRST : FIRST + out_rows])


def first_kernel(
    rows, win, wins, feat, halo, stream, taps, filt, fh, fl, gh, gl, out, sq, xs, prod, gate
):
    total = HALO + rows
    seg = (total - 8) // SEGS
    unroll = 5 if seg % 5 == 0 else 1

    for g in range(2):
        lanes = slice(g * 128, g * 128 + 128)
        for f in range(3):
            xs[f, HALO:total, :] = feat[f, :, lanes].astype(f32)
        xs[0, HALO - 16 : HALO, :] = halo[2 * HALO : 2 * HALO + 16, lanes].astype(f32)
        xs[1, 0:HALO, :] = halo[0:HALO, lanes].astype(f32)
        xs[2, 0:HALO, :] = halo[HALO : 2 * HALO, lanes].astype(f32)

        def step(it, carry):
            t0 = it * unroll
            made = []
            for f in range(3):
                held = [
                    xs[f, pl.ds(t0 + j + 2, SEGS, stride=seg), :] for j in range(unroll + 6)
                ]
                ws = [taps[f, k : k + 1, lanes] for k in range(TAPS)]
                made.append(
                    [sum(ws[k] * held[u + 6 - k] for k in range(TAPS)) for u in range(unroll)]
                )
            for u in range(unroll):
                prod[g, pl.ds(t0 + u + 8, SEGS, stride=seg), :] = made[1][u] * made[2][u]
                gate[g, pl.ds(t0 + u + 8, SEGS, stride=seg), :] = made[0][u]
            return carry

        lax.fori_loop(0, seg // unroll, step, 0)
        prod[g, 0:8, :] = jnp.zeros((8, 128), f32)
        tail = (wins - 1) * win + NFFT
        if tail > total:
            prod[g, total:tail, :] = jnp.zeros((tail - total, 128), f32)

    nt = (((1,), (1,)), ((), ()))
    spec = lax.dot_general(fh[:, 0:MR], filt[...], nt, preferred_element_type=f32)
    spec = spec + lax.dot_general(fl[:, 0:MR], filt[...], nt, preferred_element_type=f32)
    hr, hi = spec[:HALF], spec[HALF:]
    top = lax.broadcasted_iota(jnp.int32, hr.shape, 0) == 0
    mid = jnp.where(top, 0.0, hi)
    low = jnp.where(top, hi, hr)

    head = halo[2 * HALO + 16 : 2 * HALO + 32, :].astype(f32)[16 - LEAD :]
    for b in range(wins):
        start = win * b
        x = jnp.concatenate(
            [prod[0, start : start + NFFT, :], prod[1, start : start + NFFT, :]], axis=1
        ).astype(bf16)
        s = jnp.dot(fh[...], x, preferred_element_type=f32) + jnp.dot(
            fl[...], x, preferred_element_type=f32
        )
        sr, si = s[:HALF], s[HALF:]
        y = jnp.concatenate([hr * sr - mid * si, mid * sr + low * si], axis=0)
        yh = y.astype(bf16)
        yl = (y - yh.astype(f32)).astype(bf16)
        medium = (
            jnp.dot(gh[...], yh, preferred_element_type=f32)
            + jnp.dot(gh[...], yl, preferred_element_type=f32)
            + jnp.dot(gl[...], yh, preferred_element_type=f32)
        )[:win]
        first = FIRST + start
        gates = jnp.concatenate(
            [gate[0, first : first + win, :], gate[1, first : first + win, :]], axis=1
        )
        if b == 0:
            base = jnp.concatenate([head, stream[0 : win - LEAD, :].astype(f32)], axis=0)
        else:
            base = stream[start - LEAD : start - LEAD + win, :].astype(f32)
        value = base + gates * medium
        out[start : start + win, :] = value
        squared = value * value
        part = squared[:, :128] + squared[:, 128:]

        @pl.when(pl.program_id(0) == 0)
        def _():
            sq[start : start + win, :] = part

        @pl.when(pl.program_id(0) > 0)
        def _():
            sq[start : start + win, :] = sq[start : start + win, :] + part


def second_kernel(seg, stream, scale, gain, taps, decay, ends, prod, gate, states, total, nrm):
    n = seg * SEGS
    nrm[0:8, :] = jnp.zeros((8, 128), f32)
    nrm[8 : 8 + n, :] = (stream[...] * scale[...] * gain[...]).astype(bf16).astype(f32)
    unroll = 3 if seg % 3 == 0 else 1
    place = lax.broadcasted_iota(jnp.int32, (SEGS, 128), 0) * seg

    def step(it, state):
        t0 = it * unroll
        held = [nrm[pl.ds(t0 + j + 2, SEGS, stride=seg), :] for j in range(unroll + 6)]
        state = list(state)
        made = []
        for f in range(3):
            ws = [taps[f, k : k + 1, :] for k in range(TAPS)]
            made.append(
                [sum(ws[k] * held[u + 6 - k] for k in range(TAPS)) for u in range(unroll)]
            )
        values = []
        for u in range(unroll):
            p = (made[1][u] * made[2][u]).astype(bf16).astype(f32)
            p = jnp.where(place + (t0 + u) >= LEAD, p, 0.0)
            prod[t0 + u] = p
            gate[t0 + u] = made[0][u]
            values.append(p)
        for m in range(MODES):
            d = decay[m]
            for u in range(unroll):
                state[m] = state[m] * d + values[u]
        return tuple(state)

    zero = jnp.zeros((SEGS, 128), f32)
    state = lax.fori_loop(0, seg // unroll, step, (zero,) * MODES)
    for m in range(MODES):
        states[m] = state[m]
        total[m : m + 1, :] = jnp.sum(state[m] * ends[m], axis=0, keepdims=True)


def third_kernel(
    seg, count, prod, gate, states, totals, coef, stream, decay, weight, span, out, init, ybuf
):
    n = seg * SEGS
    row = coef[0] * totals[0]
    for e in range(1, count):
        row = row + coef[e] * totals[e]
    for s in range(SEGS):
        init[:, s, :] = row
        row = row * span[...] + states[:, s, :]
    unroll = 3 if seg % 3 == 0 else 1

    def step(it, state):
        t0 = it * unroll
        state = list(state)
        values = [prod[t0 + u] for u in range(unroll)]
        sums = [None] * unroll
        for m in range(MODES):
            d = decay[m]
            w = weight[m]
            for u in range(unroll):
                state[m] = state[m] * d + values[u]
                term = state[m] * w
                sums[u] = term if sums[u] is None else sums[u] + term
        for u in range(unroll):
            ybuf[pl.ds(t0 + u, SEGS, stride=seg), :] = gate[t0 + u] * sums[u]
        return tuple(state)

    lax.fori_loop(0, seg // unroll, step, tuple(init[m] for m in range(MODES)))
    out[...] = (stream[LEAD:n, :] + ybuf[LEAD:n, :]).astype(bf16)


def params():
    return pltpu.CompilerParams(
        dimension_semantics=("arbitrary",), vmem_limit_bytes=VMEM_LIMIT
    )


def body(stream_in, features, mr_taps, mr_filter, norm_gain, li_taps, modal_rates, modal_weights):
    rows, _, width = features.shape
    count = lax.axis_size("ctx")
    place = lax.axis_index("ctx")
    whole = width * lax.axis_size("tp")
    ext = rows + LEAD
    feats = jnp.transpose(features, (1, 0, 2))
    taps_one = jnp.transpose(mr_taps, (0, 2, 1))
    taps_two = jnp.transpose(li_taps, (0, 2, 1))
    rates = jnp.transpose(modal_rates)
    weights = jnp.transpose(modal_weights)

    tail = jnp.concatenate(
        [
            feats[1, rows - HALO :],
            feats[2, rows - HALO :],
            feats[0, rows - 16 :],
            stream_in[rows - 16 :],
        ],
        axis=0,
    )
    halo = lax.ppermute(tail, "ctx", [(i, i + 1) for i in range(count - 1)])

    wins = next(w for w in range(1, ext) if ext % w == 0 and (ext // w) % 8 == 0 and ext // w + FIRST <= NFFT)
    win = ext // wins
    padded = -(-win // 16) * 16
    (fh, fl), (gh, gl) = dft_tables(padded)
    total_rows = HALO + rows
    buf = max(total_rows, (wins - 1) * win + NFFT)
    cb = 256
    full = lambda shape: pl.BlockSpec(shape, lambda j: (0,) * len(shape))
    stream, squares = pl.pallas_call(
        functools.partial(first_kernel, rows, win, wins),
        grid=(width // cb,),
        in_specs=[
            pl.BlockSpec((3, rows, cb), lambda j: (0, 0, j)),
            pl.BlockSpec((2 * HALO + 32, cb), lambda j: (0, j)),
            pl.BlockSpec((rows, cb), lambda j: (0, j)),
            pl.BlockSpec((3, TAPS, cb), lambda j: (0, 0, j)),
            pl.BlockSpec((cb, MR), lambda j: (j, 0)),
            full((NFFT, NFFT)),
            full((NFFT, NFFT)),
            full((padded, NFFT)),
            full((padded, NFFT)),
        ],
        out_specs=[
            pl.BlockSpec((ext, cb), lambda j: (0, j)),
            pl.BlockSpec((ext, 128), lambda j: (0, 0)),
        ],
        out_shape=[
            jax.ShapeDtypeStruct((ext, width), f32),
            jax.ShapeDtypeStruct((ext, 128), f32),
        ],
        scratch_shapes=[
            pltpu.VMEM((3, total_rows, 128), f32),
            pltpu.VMEM((2, buf, 128), f32),
            pltpu.VMEM((2, total_rows, 128), f32),
        ],
        compiler_params=params(),
        name="medium",
    )(feats, halo, stream_in, taps_one, mr_filter, jnp.asarray(fh), jnp.asarray(fl), jnp.asarray(gh), jnp.asarray(gl))

    squares = lax.psum(jnp.sum(squares, axis=1), "tp")
    scale = jnp.broadcast_to(lax.rsqrt(squares / whole + EPS)[:, None], (ext, 128))

    seg = ext // SEGS
    decay = jnp.broadcast_to(jnp.exp(-rates)[:, None, :], (MODES, SEGS, width))
    scaled = weights * jnp.sqrt(-jnp.expm1(-2.0 * rates))
    weight = jnp.broadcast_to(scaled[:, None, :], (MODES, SEGS, width))
    left = (SEGS - 1 - jnp.arange(SEGS, dtype=f32)) * seg
    ends = jnp.exp(-rates[:, None, :] * left[None, :, None])
    span = jnp.exp(-rates * seg)
    apart = place - 1 - jnp.arange(count)
    coef = jnp.where(
        (apart >= 0)[:, None, None],
        jnp.exp(-rates[None] * (jnp.maximum(apart, 0) * rows - LEAD).astype(f32)[:, None, None]),
        0.0,
    )
    col = lambda *lead: pl.BlockSpec(lead + (128,), lambda j: (0,) * len(lead) + (j,))
    prod, gate, states, total = pl.pallas_call(
        functools.partial(second_kernel, seg),
        grid=(width // 128,),
        in_specs=[
            col(ext),
            full((ext, 128)),
            col(1),
            col(3, TAPS),
            col(MODES, SEGS),
            col(MODES, SEGS),
        ],
        out_specs=[col(seg, SEGS), col(seg, SEGS), col(MODES, SEGS), col(MODES)],
        out_shape=[
            jax.ShapeDtypeStruct((seg, SEGS, width), f32),
            jax.ShapeDtypeStruct((seg, SEGS, width), f32),
            jax.ShapeDtypeStruct((MODES, SEGS, width), f32),
            jax.ShapeDtypeStruct((MODES, width), f32),
        ],
        scratch_shapes=[pltpu.VMEM((8 + ext, 128), f32)],
        compiler_params=params(),
        name="states",
    )(stream, scale, norm_gain[None, :], taps_two, decay, ends)

    totals = lax.all_gather(total, "ctx")

    return pl.pallas_call(
        functools.partial(third_kernel, seg, count),
        grid=(width // 128,),
        in_specs=[
            col(seg, SEGS),
            col(seg, SEGS),
            col(MODES, SEGS),
            col(count, MODES),
            col(count, MODES),
            col(ext),
            col(MODES, SEGS),
            col(MODES, SEGS),
            col(MODES),
        ],
        out_specs=col(rows),
        out_shape=jax.ShapeDtypeStruct((rows, width), bf16),
        scratch_shapes=[pltpu.VMEM((MODES, SEGS, 128), f32), pltpu.VMEM((ext, 128), f32)],
        compiler_params=params(),
        name="mix",
    )(prod, gate, states, totals, coef, stream, decay, weight, span)


def solution(mesh):
    in_specs = (
        P("ctx", "tp"),
        P("ctx", None, "tp"),
        P(None, "tp", None),
        P("tp", None),
        P("tp"),
        P(None, "tp", None),
        P("tp", None),
        P("tp", None),
    )
    return jax.shard_map(
        body, mesh=mesh, in_specs=in_specs, out_specs=P("ctx", "tp"), check_vma=False
    )
```

```python
import functools

import jax
import jax.numpy as jnp
import ml_dtypes
import numpy as np
from jax import lax
from jax.experimental import pallas as pl
from jax.experimental.pallas import tpu as pltpu
from jax.sharding import PartitionSpec as P

EPS = 1e-06
MODES = 16
TAPS = 7
MR = 128
HALO = 144
LEAD = 8
SEGS = 8
NFFT = 512
HALF = NFFT // 2
FIRST = HALO - LEAD
VMEM_LIMIT = 60 * 1024 * 1024
f32 = jnp.float32
bf16 = jnp.bfloat16


def split_np(matrix):
    high = matrix.astype(np.float32).astype(ml_dtypes.bfloat16)
    low = (matrix - high.astype(np.float64)).astype(np.float32).astype(ml_dtypes.bfloat16)
    return high, low


def dft_tables(out_rows):
    k = np.arange(HALF)[:, None]
    i = np.arange(NFFT)[None, :]
    angle = 2.0 * np.pi * ((k * i) % NFFT) / NFFT
    sign = 1.0 - 2.0 * (i % 2)
    forward = np.concatenate([np.cos(angle), -np.sin(angle)], axis=0)
    forward[HALF] = sign[0]
    back = 2.0 * forward.T / NFFT
    back[:, 0] *= 0.5
    back[:, HALF] *= 0.5
    return split_np(forward), split_np(back[FIRST : FIRST + out_rows])


def steps(count, unroll, step, carry):
    main = count // unroll
    carry = lax.fori_loop(0, main, lambda it, c: step(it * unroll, unroll, c), carry)
    if count % unroll:
        carry = step(main * unroll, count % unroll, carry)
    return carry


def tree(terms):
    while len(terms) > 1:
        terms = [sum(terms[i + 1 : i + 2], terms[i]) for i in range(0, len(terms), 2)]
    return terms[0]


def first_kernel(
    rows, win, wins, begin, feat, halo, stream, taps, filt, fh, fl, g_mat, out, sq, xs, prod, gate
):
    low_row = 8 if begin == 0 else begin
    last = (begin // win + wins - 1) * win
    high = min(HALO + rows, last + FIRST + win if begin == 0 else HALO + rows)
    base_x = low_row - 8
    seg = (high - low_row) // SEGS
    tail = last + NFFT

    for g in range(2):
        lanes = slice(g * 128, g * 128 + 128)
        if begin == 0:
            own = high - HALO
            own16 = -(-own // 16) * 16
            for f in range(3):
                xs[f, HALO : HALO + own16, :] = feat[f, 0:own16, lanes].astype(f32)
            xs[0, HALO - 16 : HALO, :] = halo[2 * HALO : 2 * HALO + 16, lanes].astype(f32)
            xs[1, 0:HALO, :] = halo[0:HALO, lanes].astype(f32)
            xs[2, 0:HALO, :] = halo[HALO : 2 * HALO, lanes].astype(f32)
            shift = 0
        else:
            skip = (base_x - HALO) // 16 * 16
            shift = base_x - HALO - skip
            for f in range(3):
                xs[f, 0 : rows - skip, :] = feat[f, skip:rows, lanes].astype(f32)

        def step(t0, n, carry):
            made = []
            for f in range(3):
                held = [xs[f, pl.ds(t0 + j + 2 + shift, SEGS, stride=seg), :] for j in range(n + 6)]
                ws = [taps[f, k : k + 1, lanes] for k in range(TAPS)]
                made.append([tree([ws[k] * held[u + 6 - k] for k in range(TAPS)]) for u in range(n)])
            for u in range(n):
                at = pl.ds(t0 + u + low_row - begin, SEGS, stride=seg)
                prod[g, at, :] = made[1][u] * made[2][u]
                gate[g, at, :] = made[0][u]
            return carry

        steps(seg, 6, step, 0)
        if low_row > begin:
            prod[g, 0 : low_row - begin, :] = jnp.zeros((low_row - begin, 128), f32)
        if tail > high:
            prod[g, high - begin : tail - begin, :] = jnp.zeros((tail - high, 128), f32)

    nt = (((1,), (1,)), ((), ()))
    spec = lax.dot_general(fh[:, 0:MR], filt[...], nt, preferred_element_type=f32)
    spec = spec + lax.dot_general(fl[:, 0:MR], filt[...], nt, preferred_element_type=f32)
    hr, hi = spec[:HALF], spec[HALF:]
    top = lax.broadcasted_iota(jnp.int32, hr.shape, 0) == 0
    mid = jnp.where(top, 0.0, hi)
    low = jnp.where(top, hi, hr)

    for b in range(wins):
        start = win * b
        x = jnp.concatenate(
            [prod[0, start : start + NFFT, :], prod[1, start : start + NFFT, :]], axis=1
        ).astype(bf16)
        s = jnp.dot(fh[...], x, preferred_element_type=f32)
        sr, si = s[:HALF], s[HALF:]
        y = jnp.concatenate(
            [(hr * sr - mid * si).astype(bf16), (mid * sr + low * si).astype(bf16)], axis=0
        )
        medium = jnp.dot(g_mat[...], y, preferred_element_type=f32)[:win]
        first = FIRST + start
        gates = jnp.concatenate(
            [gate[0, first : first + win, :], gate[1, first : first + win, :]], axis=1
        )
        if begin == 0 and b == 0:
            head = halo[2 * HALO + 16 : 2 * HALO + 32, :].astype(f32)[16 - LEAD :]
            base = jnp.concatenate([head, stream[0 : win - LEAD, :].astype(f32)], axis=0)
        else:
            base = stream[begin + start - LEAD : begin + start - LEAD + win, :].astype(f32)
        value = base + gates * medium
        out[start : start + win, :] = value
        squared = value * value
        part = squared[:, :128] + squared[:, 128:]

        @pl.when(pl.program_id(0) == 0)
        def _():
            sq[start : start + win, :] = part

        @pl.when(pl.program_id(0) > 0)
        def _():
            sq[start : start + win, :] = sq[start : start + win, :] + part


def second_kernel(
    seg, count, near, far, scale, gain, taps, decay, ends,
    prod, gate, states, gathered, nrm, held_total, send_sem, recv_sem,
):
    n = seg * SEGS
    me = lax.axis_index("ctx")
    group = pl.program_id(0)
    groups = held_total.shape[0]

    def peer_copy(g, k):
        return pltpu.make_async_remote_copy(
            src_ref=held_total.at[g],
            dst_ref=gathered.at[g, me],
            send_sem=send_sem.at[g, k - 1],
            recv_sem=recv_sem.at[g, k - 1],
            device_id={"ctx": lax.rem(me + k, count)},
            device_id_type=pl.DeviceIdType.MESH,
        )

    @pl.when(group == 0)
    def _():
        barrier = pltpu.get_barrier_semaphore()

        def greet(k, c):
            pl.semaphore_signal(
                barrier, inc=1, device_id={"ctx": lax.rem(me + k, count)},
                device_id_type=pl.DeviceIdType.MESH,
            )
            return c

        lax.fori_loop(1, count, greet, 0)
        pl.semaphore_wait(barrier, count - 1)

    cut = near.shape[0]
    nrm[0:8, :] = jnp.zeros((8, 128), f32)
    nrm[8 : 8 + cut, :] = (near[...] * scale[0:cut, :] * gain[...]).astype(bf16).astype(f32)
    nrm[8 + cut : 8 + n, :] = (far[...] * scale[cut:n, :] * gain[...]).astype(bf16).astype(f32)
    place = lax.broadcasted_iota(jnp.int32, (SEGS, 128), 0) * seg

    def step(t0, size, state):
        held = [nrm[pl.ds(t0 + j + 2, SEGS, stride=seg), :] for j in range(size + 6)]
        state = list(state)
        made = []
        for f in range(3):
            ws = [taps[f, k : k + 1, :] for k in range(TAPS)]
            made.append([tree([ws[k] * held[u + 6 - k] for k in range(TAPS)]) for u in range(size)])
        values = []
        for u in range(size):
            p = (made[1][u] * made[2][u]).astype(bf16).astype(f32)
            p = jnp.where(place + (t0 + u) >= LEAD, p, 0.0)
            prod[t0 + u] = p
            gate[t0 + u] = made[0][u]
            values.append(p)
        for m in range(MODES):
            d = decay[m]
            for u in range(size):
                state[m] = state[m] * d + values[u]
        return tuple(state)

    zero = jnp.zeros((SEGS, 128), f32)
    state = steps(seg, 6, step, (zero,) * MODES)
    for m in range(MODES):
        states[m] = state[m]
        held_total[group, m : m + 1, :] = jnp.sum(state[m] * ends[m], axis=0, keepdims=True)

    def send(k, c):
        @pl.when(me + k < count)
        def _():
            peer_copy(group, k).start()

        return c

    lax.fori_loop(1, count, send, 0)

    @pl.when(group == groups - 1)
    def _():
        def finish(at, c):
            g, k = at // (count - 1), at % (count - 1) + 1

            @pl.when(me + k < count)
            def _():
                peer_copy(g, k).wait_send()

            @pl.when(me - k >= 0)
            def _():
                peer_copy(g, k).wait_recv()

            return c

        lax.fori_loop(0, groups * (count - 1), finish, 0)


def third_kernel(
    seg, count, prod, gate, states, totals, coef, near, far, decay, weight, span, out, init, ybuf
):
    n = seg * SEGS
    row = jnp.zeros(span.shape, f32)
    for e in range(count):
        row = row + jnp.where(coef[e] == 0.0, 0.0, coef[e] * totals[0, e])
    for s in range(SEGS):
        init[:, s, :] = row
        row = row * span[...] + states[:, s, :]

    def step(t0, size, state):
        state = list(state)
        values = [prod[t0 + u] for u in range(size)]
        sums = [[None] * 2 for _ in range(size)]
        for m in range(MODES):
            d = decay[m]
            w = weight[m]
            for u in range(size):
                state[m] = state[m] * d + values[u]
                term = state[m] * w
                had = sums[u][m % 2]
                sums[u][m % 2] = term if had is None else had + term
        for u in range(size):
            ybuf[pl.ds(t0 + u, SEGS, stride=seg), :] = gate[t0 + u] * (sums[u][0] + sums[u][1])
        return tuple(state)

    steps(seg, 8, step, tuple(init[m] for m in range(MODES)))
    cut = near.shape[0]
    out[0 : cut - LEAD, :] = (near[LEAD:cut, :] + ybuf[LEAD:cut, :]).astype(bf16)
    out[cut - LEAD : n - LEAD, :] = (far[...] + ybuf[cut:n, :]).astype(bf16)


def params(**more):
    return pltpu.CompilerParams(
        dimension_semantics=("arbitrary",), vmem_limit_bytes=VMEM_LIMIT, **more
    )


def body(stream_in, features, mr_taps, mr_filter, norm_gain, li_taps, modal_rates, modal_weights):
    rows, _, width = features.shape
    count = lax.axis_size("ctx")
    place = lax.axis_index("ctx")
    whole = width * lax.axis_size("tp")
    ext = rows + LEAD
    feats = jnp.transpose(features, (1, 0, 2))
    taps_one = jnp.transpose(mr_taps, (0, 2, 1))
    taps_two = jnp.transpose(li_taps, (0, 2, 1))
    rates = jnp.transpose(modal_rates)
    weights = jnp.transpose(modal_weights)

    tail = jnp.concatenate(
        [
            feats[1, rows - HALO :],
            feats[2, rows - HALO :],
            feats[0, rows - 16 :],
            stream_in[rows - 16 :],
        ],
        axis=0,
    )
    halo = lax.ppermute(tail, "ctx", [(i, i + 1) for i in range(count - 1)])

    wins = next(w for w in range(1, ext) if ext % w == 0 and (ext // w) % 8 == 0 and ext // w + FIRST <= NFFT)
    win = ext // wins
    padded = -(-win // 16) * 16
    (fh, fl), (gh, gl) = dft_tables(padded)
    cb = 256
    full = lambda shape: pl.BlockSpec(shape, lambda j: (0,) * len(shape))
    fh, fl, g_mat = jnp.asarray(fh), jnp.asarray(fl), jnp.asarray(gh)

    def medium(begin, count_wins, halo):
        out_rows = win * count_wins
        buf = max(HALO + rows - begin, (count_wins - 1) * win + NFFT)
        return pl.pallas_call(
            functools.partial(first_kernel, rows, win, count_wins, begin),
            grid=(width // cb,),
            in_specs=[
                pl.BlockSpec((3, rows, cb), lambda j: (0, 0, j)),
                pl.BlockSpec((halo.shape[0], cb), lambda j: (0, j)),
                pl.BlockSpec((rows, cb), lambda j: (0, j)),
                pl.BlockSpec((3, TAPS, cb), lambda j: (0, 0, j)),
                pl.BlockSpec((cb, MR), lambda j: (j, 0)),
                full((NFFT, NFFT)),
                full((NFFT, NFFT)),
                full((padded, NFFT)),
            ],
            out_specs=[
                pl.BlockSpec((out_rows, cb), lambda j: (0, j)),
                pl.BlockSpec((out_rows, 128), lambda j: (0, 0)),
            ],
            out_shape=[
                jax.ShapeDtypeStruct((out_rows, width), f32),
                jax.ShapeDtypeStruct((out_rows, 128), f32),
            ],
            scratch_shapes=[
                pltpu.VMEM((3, HALO + rows, 128), f32),
                pltpu.VMEM((2, buf, 128), f32),
                pltpu.VMEM((2, buf, 128), f32),
            ],
            compiler_params=params(),
            cost_estimate=pl.CostEstimate(
                flops=12_000_000_000 * count_wins, bytes_accessed=20_000_000 * count_wins, transcendentals=0
            ),
            name="medium_head" if begin == 0 else "medium_rest",
        )(feats, halo, stream_in, taps_one, mr_filter, fh, fl, g_mat)

    far, far_squares = medium(win, wins - 1, stream_in[:16])
    near, near_squares = medium(0, 1, halo)
    squares = jnp.concatenate([jnp.sum(near_squares, axis=1), jnp.sum(far_squares, axis=1)])

    squares = lax.psum(squares, "tp")
    scale = jnp.broadcast_to(lax.rsqrt(squares / whole + EPS)[:, None], (ext, 128))

    seg = ext // SEGS
    decay = jnp.broadcast_to(jnp.exp(-rates)[:, None, :], (MODES, SEGS, width))
    scaled = weights * jnp.sqrt(-jnp.expm1(-2.0 * rates))
    weight = jnp.broadcast_to(scaled[:, None, :], (MODES, SEGS, width))
    left = (SEGS - 1 - jnp.arange(SEGS, dtype=f32)) * seg
    ends = jnp.exp(-rates[:, None, :] * left[None, :, None])
    span = jnp.exp(-rates * seg)
    apart = place - 1 - jnp.arange(count)
    coef = jnp.where(
        (apart >= 0)[:, None, None],
        jnp.exp(-rates[None] * (jnp.maximum(apart, 0) * rows - LEAD).astype(f32)[:, None, None]),
        0.0,
    )
    col = lambda *lead: pl.BlockSpec(lead + (128,), lambda j: (0,) * len(lead) + (j,))
    groups = width // 128
    prod, gate, states, totals = pl.pallas_call(
        functools.partial(second_kernel, seg, count),
        grid=(width // 128,),
        in_specs=[
            col(win),
            col(ext - win),
            full((ext, 128)),
            col(1),
            col(3, TAPS),
            col(MODES, SEGS),
            col(MODES, SEGS),
        ],
        out_specs=[col(seg, SEGS), col(seg, SEGS), col(MODES, SEGS), pl.BlockSpec(memory_space=pl.ANY)],
        out_shape=[
            jax.ShapeDtypeStruct((seg, SEGS, width), f32),
            jax.ShapeDtypeStruct((seg, SEGS, width), f32),
            jax.ShapeDtypeStruct((MODES, SEGS, width), f32),
            jax.ShapeDtypeStruct((groups, count, MODES, 128), f32),
        ],
        scratch_shapes=[
            pltpu.VMEM((8 + ext, 128), f32),
            pltpu.VMEM((groups, MODES, 128), f32),
            pltpu.SemaphoreType.DMA((groups, count - 1)),
            pltpu.SemaphoreType.DMA((groups, count - 1)),
        ],
        compiler_params=params(collective_id=0, has_side_effects=True),
        name="states",
    )(near, far, scale, norm_gain[None, :], taps_two, decay, ends)

    return pl.pallas_call(
        functools.partial(third_kernel, seg, count),
        grid=(width // 128,),
        in_specs=[
            col(seg, SEGS),
            col(seg, SEGS),
            col(MODES, SEGS),
            pl.BlockSpec((1, count, MODES, 128), lambda j: (j, 0, 0, 0)),
            col(count, MODES),
            col(win),
            col(ext - win),
            col(MODES, SEGS),
            col(MODES, SEGS),
            col(MODES),
        ],
        out_specs=col(rows),
        out_shape=jax.ShapeDtypeStruct((rows, width), bf16),
        scratch_shapes=[pltpu.VMEM((MODES, SEGS, 128), f32), pltpu.VMEM((ext, 128), f32)],
        compiler_params=params(),
        name="mix",
    )(prod, gate, states, totals, coef, near, far, decay, weight, span)


def solution(mesh):
    in_specs = (
        P("ctx", "tp"),
        P("ctx", None, "tp"),
        P(None, "tp", None),
        P("tp", None),
        P("tp"),
        P(None, "tp", None),
        P("tp", None),
        P("tp", None),
    )
    return jax.shard_map(
        body, mesh=mesh, in_specs=in_specs, out_specs=P("ctx", "tp"), check_vma=False
    )
```

```python
import functools

import jax
import jax.numpy as jnp
import ml_dtypes
import numpy as np
from jax import lax
from jax.experimental import pallas as pl
from jax.experimental.pallas import tpu as pltpu
from jax.sharding import PartitionSpec as P

EPS = 1e-06
MODES = 16
TAPS = 7
MR = 128
HALO = 144
LEAD = 8
SEGS = 8
NFFT = 512
HALF = NFFT // 2
FIRST = HALO - LEAD
VMEM_LIMIT = 60 * 1024 * 1024
f32 = jnp.float32
bf16 = jnp.bfloat16


def split_np(matrix):
    high = matrix.astype(np.float32).astype(ml_dtypes.bfloat16)
    low = (matrix - high.astype(np.float64)).astype(np.float32).astype(ml_dtypes.bfloat16)
    return high, low


def dft_tables(out_rows):
    k = np.arange(HALF)[:, None]
    i = np.arange(NFFT)[None, :]
    angle = 2.0 * np.pi * ((k * i) % NFFT) / NFFT
    sign = 1.0 - 2.0 * (i % 2)
    forward = np.concatenate([np.cos(angle), -np.sin(angle)], axis=0)
    forward[HALF] = sign[0]
    back = 2.0 * forward.T / NFFT
    back[:, 0] *= 0.5
    back[:, HALF] *= 0.5
    return split_np(forward), split_np(back[FIRST : FIRST + out_rows])


def steps(count, unroll, step, carry):
    main = count // unroll
    carry = lax.fori_loop(0, main, lambda it, c: step(it * unroll, unroll, c), carry)
    if count % unroll:
        carry = step(main * unroll, count % unroll, carry)
    return carry


def tree(terms):
    while len(terms) > 1:
        terms = [sum(terms[i + 1 : i + 2], terms[i]) for i in range(0, len(terms), 2)]
    return terms[0]


def first_kernel(
    rows, win, wins, begin, feat, halo, stream, taps, filt, fh, fl, g_mat, out, sq, xs, prod, gate
):
    low_row = 8 if begin == 0 else begin
    last = (begin // win + wins - 1) * win
    high = min(HALO + rows, last + FIRST + win if begin == 0 else HALO + rows)
    base_x = low_row - 8
    seg = (high - low_row) // SEGS
    tail = last + NFFT

    for g in range(2):
        lanes = slice(g * 128, g * 128 + 128)
        if begin == 0:
            own = high - HALO
            own16 = -(-own // 16) * 16
            for f in range(3):
                xs[f, HALO : HALO + own16, :] = feat[f, 0:own16, lanes].astype(f32)
            xs[0, HALO - 16 : HALO, :] = halo[2 * HALO : 2 * HALO + 16, lanes].astype(f32)
            xs[1, 0:HALO, :] = halo[0:HALO, lanes].astype(f32)
            xs[2, 0:HALO, :] = halo[HALO : 2 * HALO, lanes].astype(f32)
            shift = 0
        else:
            skip = (base_x - HALO) // 16 * 16
            shift = base_x - HALO - skip
            for f in range(3):
                xs[f, 0 : rows - skip, :] = feat[f, skip:rows, lanes].astype(f32)

        def step(t0, n, carry):
            made = []
            for f in range(3):
                held = [xs[f, pl.ds(t0 + j + 2 + shift, SEGS, stride=seg), :] for j in range(n + 6)]
                ws = [taps[f, k : k + 1, lanes] for k in range(TAPS)]
                made.append([tree([ws[k] * held[u + 6 - k] for k in range(TAPS)]) for u in range(n)])
            for u in range(n):
                at = pl.ds(t0 + u + low_row - begin, SEGS, stride=seg)
                prod[g, at, :] = made[1][u] * made[2][u]
                gate[g, at, :] = made[0][u]
            return carry

        steps(seg, 6, step, 0)
        if low_row > begin:
            prod[g, 0 : low_row - begin, :] = jnp.zeros((low_row - begin, 128), f32)
        if tail > high:
            prod[g, high - begin : tail - begin, :] = jnp.zeros((tail - high, 128), f32)

    nt = (((1,), (1,)), ((), ()))
    spec = lax.dot_general(fh[:, 0:MR], filt[...], nt, preferred_element_type=f32)
    spec = spec + lax.dot_general(fl[:, 0:MR], filt[...], nt, preferred_element_type=f32)
    hr, hi = spec[:HALF], spec[HALF:]
    top = lax.broadcasted_iota(jnp.int32, hr.shape, 0) == 0
    mid = jnp.where(top, 0.0, hi)
    low = jnp.where(top, hi, hr)

    for b in range(wins):
        start = win * b
        x = jnp.concatenate(
            [prod[0, start : start + NFFT, :], prod[1, start : start + NFFT, :]], axis=1
        ).astype(bf16)
        s = jnp.dot(fh[...], x, preferred_element_type=f32)
        sr, si = s[:HALF], s[HALF:]
        y = jnp.concatenate(
            [(hr * sr - mid * si).astype(bf16), (mid * sr + low * si).astype(bf16)], axis=0
        )
        medium = jnp.dot(g_mat[...], y, preferred_element_type=f32)[:win]
        first = FIRST + start
        gates = jnp.concatenate(
            [gate[0, first : first + win, :], gate[1, first : first + win, :]], axis=1
        )
        if begin == 0 and b == 0:
            head = halo[2 * HALO + 16 : 2 * HALO + 32, :].astype(f32)[16 - LEAD :]
            base = jnp.concatenate([head, stream[0 : win - LEAD, :].astype(f32)], axis=0)
        else:
            base = stream[begin + start - LEAD : begin + start - LEAD + win, :].astype(f32)
        value = base + gates * medium
        out[start : start + win, :] = value
        squared = value * value
        part = squared[:, :128] + squared[:, 128:]

        @pl.when(pl.program_id(0) == 0)
        def _():
            sq[start : start + win, :] = part

        @pl.when(pl.program_id(0) > 0)
        def _():
            sq[start : start + win, :] = sq[start : start + win, :] + part


def second_kernel(
    seg, count, lanes_count, whole, near, far, near_sq, far_sq, gain, taps, rates,
    prod, gate, states, gathered, nrm, held_total, send_sem, recv_sem,
    parts, sums, scale, sum_send, sum_recv, decay,
):
    n = seg * SEGS
    me = lax.axis_index("ctx")
    group = pl.program_id(0)
    groups = held_total.shape[0]

    def peer_copy(g, k):
        return pltpu.make_async_remote_copy(
            src_ref=held_total.at[g],
            dst_ref=gathered.at[g, me],
            send_sem=send_sem.at[g, k - 1],
            recv_sem=recv_sem.at[g, k - 1],
            device_id={"ctx": lax.rem(me + k, count)},
            device_id_type=pl.DeviceIdType.MESH,
        )

    @pl.when(group == 0)
    def _():
        barrier = pltpu.get_barrier_semaphore()

        def greet(k, c):
            pl.semaphore_signal(
                barrier, inc=1, device_id={"ctx": lax.rem(me + k, count)},
                device_id_type=pl.DeviceIdType.MESH,
            )
            return c

        lax.fori_loop(1, count, greet, 0)
        mine = lax.axis_index("tp")
        for k in range(1, lanes_count):
            pl.semaphore_signal(
                barrier, inc=1, device_id={"tp": lax.rem(mine + k, lanes_count)},
                device_id_type=pl.DeviceIdType.MESH,
            )
        pl.semaphore_wait(barrier, count - 1 + lanes_count - 1)

        half = near_sq.shape[0]
        scale[0:half, :] = near_sq[...]
        scale[half:n, :] = far_sq[...]
        scale[n:, :] = jnp.zeros((scale.shape[0] - n, 128), f32)
        parts[0] = lax.dot_general(
            jnp.ones((8, 128), f32), scale[...], (((1,), (1,)), ((), ())),
            precision=lax.Precision.HIGHEST, preferred_element_type=f32,
        )
        copies = [
            pltpu.make_async_remote_copy(
                src_ref=parts.at[0],
                dst_ref=parts.at[k],
                send_sem=sum_send.at[k - 1],
                recv_sem=sum_recv.at[k - 1],
                device_id={"tp": lax.rem(mine + k, lanes_count)},
                device_id_type=pl.DeviceIdType.MESH,
            )
            for k in range(1, lanes_count)
        ]
        for copy in copies:
            copy.start()
        for copy in copies:
            copy.wait()
        sums[...] = parts[0]
        for k in range(1, lanes_count):
            sums[...] = sums[...] + parts[k]
        column = lax.dot_general(
            sums[...], jnp.full((8, 128), 0.125, f32), (((0,), (0,)), ((), ())),
            precision=lax.Precision.HIGHEST, preferred_element_type=f32,
        )
        scale[...] = lax.rsqrt(column / whole + EPS)

    cut = near.shape[0]
    nrm[0:8, :] = jnp.zeros((8, 128), f32)
    nrm[8 : 8 + cut, :] = (near[...] * scale[0:cut, :] * gain[...]).astype(bf16).astype(f32)
    nrm[8 + cut : 8 + n, :] = (far[...] * scale[cut:n, :] * gain[...]).astype(bf16).astype(f32)
    place = lax.broadcasted_iota(jnp.int32, (SEGS, 128), 0) * seg
    left = ((SEGS - 1) * seg - place).astype(f32)
    decay[...] = jnp.exp(-rates[...])

    def step(t0, size, state):
        held = [nrm[pl.ds(t0 + j + 2, SEGS, stride=seg), :] for j in range(size + 6)]
        state = list(state)
        made = []
        for f in range(3):
            ws = [taps[f, k : k + 1, :] for k in range(TAPS)]
            made.append([tree([ws[k] * held[u + 6 - k] for k in range(TAPS)]) for u in range(size)])
        values = []
        for u in range(size):
            p = (made[1][u] * made[2][u]).astype(bf16).astype(f32)
            p = jnp.where(place + (t0 + u) >= LEAD, p, 0.0)
            prod[t0 + u] = p
            gate[t0 + u] = made[0][u]
            values.append(p)
        for m in range(MODES):
            d = decay[m : m + 1, :]
            for u in range(size):
                state[m] = state[m] * d + values[u]
        return tuple(state)

    zero = jnp.zeros((SEGS, 128), f32)
    state = steps(seg, 6, step, (zero,) * MODES)
    for m in range(MODES):
        states[m] = state[m]
        held_total[group, m : m + 1, :] = jnp.sum(
            state[m] * jnp.exp(-rates[m : m + 1, :] * left), axis=0, keepdims=True
        )

    def send(k, c):
        @pl.when(me + k < count)
        def _():
            peer_copy(group, k).start()

        return c

    lax.fori_loop(1, count, send, 0)

    @pl.when(group == groups - 1)
    def _():
        def finish(at, c):
            g, k = at // (count - 1), at % (count - 1) + 1

            @pl.when(me + k < count)
            def _():
                peer_copy(g, k).wait_send()

            @pl.when(me - k >= 0)
            def _():
                peer_copy(g, k).wait_recv()

            return c

        lax.fori_loop(0, groups * (count - 1), finish, 0)


def third_kernel(
    seg, count, prod, gate, states, totals, lags, near, far, rates, weight, out, init, ybuf, decay
):
    n = seg * SEGS
    r = rates[...]
    decay[...] = jnp.exp(-r)
    span = jnp.exp(-r * seg)
    row = jnp.zeros(r.shape, f32)
    for e in range(count):
        lag = lags[e : e + 1, :]
        used = jnp.broadcast_to(lag, r.shape) > -2.0 * LEAD
        coef = jnp.exp(-r * jnp.maximum(lag, float(-LEAD)))
        row = row + jnp.where(used, coef * totals[0, e], 0.0)
    for s in range(SEGS):
        init[:, s, :] = row
        row = row * span + states[:, s, :]

    def step(t0, size, state):
        state = list(state)
        values = [prod[t0 + u] for u in range(size)]
        sums = [[None] * 2 for _ in range(size)]
        for m in range(MODES):
            d = decay[m : m + 1, :]
            w = weight[m : m + 1, :]
            for u in range(size):
                state[m] = state[m] * d + values[u]
                term = state[m] * w
                had = sums[u][m % 2]
                sums[u][m % 2] = term if had is None else had + term
        for u in range(size):
            ybuf[pl.ds(t0 + u, SEGS, stride=seg), :] = gate[t0 + u] * (sums[u][0] + sums[u][1])
        return tuple(state)

    steps(seg, 8, step, tuple(init[m] for m in range(MODES)))
    cut = near.shape[0]
    out[0 : cut - LEAD, :] = (near[LEAD:cut, :] + ybuf[LEAD:cut, :]).astype(bf16)
    out[cut - LEAD : n - LEAD, :] = (far[...] + ybuf[cut:n, :]).astype(bf16)


def params(**more):
    return pltpu.CompilerParams(
        dimension_semantics=("arbitrary",), vmem_limit_bytes=VMEM_LIMIT, **more
    )


def body(stream_in, features, mr_taps, mr_filter, norm_gain, li_taps, modal_rates, modal_weights):
    rows, _, width = features.shape
    count = lax.axis_size("ctx")
    place = lax.axis_index("ctx")
    whole = width * lax.axis_size("tp")
    ext = rows + LEAD
    feats = jnp.transpose(features, (1, 0, 2))
    taps_one = jnp.transpose(mr_taps, (0, 2, 1))
    taps_two = jnp.transpose(li_taps, (0, 2, 1))
    rates = jnp.transpose(modal_rates)
    weights = jnp.transpose(modal_weights)

    tail = jnp.concatenate(
        [
            feats[1, rows - HALO :],
            feats[2, rows - HALO :],
            feats[0, rows - 16 :],
            stream_in[rows - 16 :],
        ],
        axis=0,
    )
    halo = lax.ppermute(tail, "ctx", [(i, i + 1) for i in range(count - 1)])

    wins = next(w for w in range(1, ext) if ext % w == 0 and (ext // w) % 8 == 0 and ext // w + FIRST <= NFFT)
    win = ext // wins
    padded = -(-win // 16) * 16
    (fh, fl), (gh, gl) = dft_tables(padded)
    cb = 256
    full = lambda shape: pl.BlockSpec(shape, lambda j: (0,) * len(shape))
    fh, fl, g_mat = jnp.asarray(fh), jnp.asarray(fl), jnp.asarray(gh)

    def medium(begin, count_wins, halo):
        out_rows = win * count_wins
        buf = max(HALO + rows - begin, (count_wins - 1) * win + NFFT)
        return pl.pallas_call(
            functools.partial(first_kernel, rows, win, count_wins, begin),
            grid=(width // cb,),
            in_specs=[
                pl.BlockSpec((3, rows, cb), lambda j: (0, 0, j)),
                pl.BlockSpec((halo.shape[0], cb), lambda j: (0, j)),
                pl.BlockSpec((rows, cb), lambda j: (0, j)),
                pl.BlockSpec((3, TAPS, cb), lambda j: (0, 0, j)),
                pl.BlockSpec((cb, MR), lambda j: (j, 0)),
                full((NFFT, NFFT)),
                full((NFFT, NFFT)),
                full((padded, NFFT)),
            ],
            out_specs=[
                pl.BlockSpec((out_rows, cb), lambda j: (0, j)),
                pl.BlockSpec((out_rows, 128), lambda j: (0, 0)),
            ],
            out_shape=[
                jax.ShapeDtypeStruct((out_rows, width), f32),
                jax.ShapeDtypeStruct((out_rows, 128), f32),
            ],
            scratch_shapes=[
                pltpu.VMEM((3, HALO + rows, 128), f32),
                pltpu.VMEM((2, buf, 128), f32),
                pltpu.VMEM((2, buf, 128), f32),
            ],
            compiler_params=params(),
            cost_estimate=pl.CostEstimate(
                flops=12_000_000_000 * count_wins, bytes_accessed=20_000_000 * count_wins, transcendentals=0
            ),
            name="medium_head" if begin == 0 else "medium_rest",
        )(feats, halo, stream_in, taps_one, mr_filter, fh, fl, g_mat)

    far, far_squares = medium(win, wins - 1, stream_in[:16])
    near, near_squares = medium(0, 1, halo)
    seg = ext // SEGS
    lanes_count = lax.axis_size("tp")
    scaled = weights * jnp.sqrt(-jnp.expm1(-2.0 * rates))
    apart = place - 1 - jnp.arange(count)
    lags = jnp.where(apart >= 0, apart * rows - LEAD, -4 * LEAD).astype(f32)
    lags = jnp.broadcast_to(lags[:, None], (count, 128))
    summed = -(-ext // 128) * 128
    col = lambda *lead: pl.BlockSpec(lead + (128,), lambda j: (0,) * len(lead) + (j,))
    groups = width // 128
    prod, gate, states, totals = pl.pallas_call(
        functools.partial(second_kernel, seg, count, lanes_count, whole),
        grid=(width // 128,),
        in_specs=[
            col(win),
            col(ext - win),
            full((win, 128)),
            full((ext - win, 128)),
            col(1),
            col(3, TAPS),
            col(MODES),
        ],
        out_specs=[col(seg, SEGS), col(seg, SEGS), col(MODES, SEGS), pl.BlockSpec(memory_space=pl.ANY)],
        out_shape=[
            jax.ShapeDtypeStruct((seg, SEGS, width), f32),
            jax.ShapeDtypeStruct((seg, SEGS, width), f32),
            jax.ShapeDtypeStruct((MODES, SEGS, width), f32),
            jax.ShapeDtypeStruct((groups, count, MODES, 128), f32),
        ],
        scratch_shapes=[
            pltpu.VMEM((8 + ext, 128), f32),
            pltpu.VMEM((groups, MODES, 128), f32),
            pltpu.SemaphoreType.DMA((groups, count - 1)),
            pltpu.SemaphoreType.DMA((groups, count - 1)),
            pltpu.VMEM((lanes_count, 8, summed), f32),
            pltpu.VMEM((8, summed), f32),
            pltpu.VMEM((summed, 128), f32),
            pltpu.SemaphoreType.DMA((lanes_count - 1,)),
            pltpu.SemaphoreType.DMA((lanes_count - 1,)),
            pltpu.VMEM((MODES, 128), f32),
        ],
        compiler_params=params(collective_id=0, has_side_effects=True),
        name="states",
    )(near, far, near_squares, far_squares, norm_gain[None, :], taps_two, rates)

    return pl.pallas_call(
        functools.partial(third_kernel, seg, count),
        grid=(width // 128,),
        in_specs=[
            col(seg, SEGS),
            col(seg, SEGS),
            col(MODES, SEGS),
            pl.BlockSpec((1, count, MODES, 128), lambda j: (j, 0, 0, 0)),
            full((count, 128)),
            col(win),
            col(ext - win),
            col(MODES),
            col(MODES),
        ],
        out_specs=col(rows),
        out_shape=jax.ShapeDtypeStruct((rows, width), bf16),
        scratch_shapes=[pltpu.VMEM((MODES, SEGS, 128), f32), pltpu.VMEM((ext, 128), f32), pltpu.VMEM((MODES, 128), f32)],
        compiler_params=params(),
        name="mix",
    )(prod, gate, states, totals, lags, near, far, rates, scaled)


def solution(mesh):
    in_specs = (
        P("ctx", "tp"),
        P("ctx", None, "tp"),
        P(None, "tp", None),
        P("tp", None),
        P("tp"),
        P(None, "tp", None),
        P("tp", None),
        P("tp", None),
    )
    return jax.shard_map(
        body, mesh=mesh, in_specs=in_specs, out_specs=P("ctx", "tp"), check_vma=False
    )
```

```python
import functools

import jax
import jax.numpy as jnp
import ml_dtypes
import numpy as np
from jax import lax
from jax.experimental import pallas as pl
from jax.experimental.pallas import tpu as pltpu
from jax.sharding import PartitionSpec as P

EPS = 1e-06
MODES = 16
TAPS = 7
MR = 128
HALO = 144
LEAD = 8
SEGS = 8
NFFT = 512
HALF = NFFT // 2
FIRST = HALO - LEAD
VMEM_LIMIT = 60 * 1024 * 1024
f32 = jnp.float32
bf16 = jnp.bfloat16


def split_np(matrix):
    high = matrix.astype(np.float32).astype(ml_dtypes.bfloat16)
    low = (matrix - high.astype(np.float64)).astype(np.float32).astype(ml_dtypes.bfloat16)
    return high, low


def dft_tables(out_rows):
    k = np.arange(HALF)[:, None]
    i = np.arange(NFFT)[None, :]
    angle = 2.0 * np.pi * ((k * i) % NFFT) / NFFT
    sign = 1.0 - 2.0 * (i % 2)
    forward = np.concatenate([np.cos(angle), -np.sin(angle)], axis=0)
    forward[HALF] = sign[0]
    back = 2.0 * forward.T / NFFT
    back[:, 0] *= 0.5
    back[:, HALF] *= 0.5
    return split_np(forward), split_np(back[FIRST : FIRST + out_rows])


def steps(count, unroll, step, carry):
    main = count // unroll
    carry = lax.fori_loop(0, main, lambda it, c: step(it * unroll, unroll, c), carry)
    if count % unroll:
        carry = step(main * unroll, count % unroll, carry)
    return carry


def tree(terms):
    while len(terms) > 1:
        terms = [sum(terms[i + 1 : i + 2], terms[i]) for i in range(0, len(terms), 2)]
    return terms[0]


def tail_kernel(rows, feats, stream, out, sems):
    copies = [
        pltpu.make_async_copy(source, out.at[place : place + size, :], sems.at[i])
        for i, (source, place, size) in enumerate(
            [
                (feats.at[1, rows - HALO : rows, :], 0, HALO),
                (feats.at[2, rows - HALO : rows, :], HALO, HALO),
                (feats.at[0, rows - 16 : rows, :], 2 * HALO, 16),
                (stream.at[rows - 16 : rows, :], 2 * HALO + 16, 16),
            ]
        )
    ]
    for copy in copies:
        copy.start()
    for copy in copies:
        copy.wait()


def first_kernel(
    rows, win, wins, begin, feat, halo, stream, taps, filt, fh, fl, g_mat, out, sq, xs, prod, gate
):
    low_row = 8 if begin == 0 else begin
    last = (begin // win + wins - 1) * win
    high = min(HALO + rows, last + FIRST + win if begin == 0 else HALO + rows)
    base_x = low_row - 8
    seg = (high - low_row) // SEGS
    tail = last + NFFT

    for g in range(2):
        lanes = slice(g * 128, g * 128 + 128)
        if begin == 0:
            own = high - HALO
            own16 = -(-own // 16) * 16
            for f in range(3):
                xs[f, HALO : HALO + own16, :] = feat[f, 0:own16, lanes].astype(f32)
            xs[0, HALO - 16 : HALO, :] = halo[2 * HALO : 2 * HALO + 16, lanes].astype(f32)
            xs[1, 0:HALO, :] = halo[0:HALO, lanes].astype(f32)
            xs[2, 0:HALO, :] = halo[HALO : 2 * HALO, lanes].astype(f32)
            shift = 0
        else:
            skip = (base_x - HALO) // 16 * 16
            shift = base_x - HALO - skip
            for f in range(3):
                xs[f, 0 : rows - skip, :] = feat[f, skip:rows, lanes].astype(f32)

        def step(t0, n, carry):
            made = []
            for f in range(3):
                held = [xs[f, pl.ds(t0 + j + 2 + shift, SEGS, stride=seg), :] for j in range(n + 6)]
                ws = [taps[f, k : k + 1, lanes] for k in range(TAPS)]
                made.append([tree([ws[k] * held[u + 6 - k] for k in range(TAPS)]) for u in range(n)])
            for u in range(n):
                at = pl.ds(t0 + u + low_row - begin, SEGS, stride=seg)
                prod[g, at, :] = made[1][u] * made[2][u]
                gate[g, at, :] = made[0][u]
            return carry

        steps(seg, 12, step, 0)
        if low_row > begin:
            prod[g, 0 : low_row - begin, :] = jnp.zeros((low_row - begin, 128), f32)
        if tail > high:
            prod[g, high - begin : tail - begin, :] = jnp.zeros((tail - high, 128), f32)

    nt = (((1,), (1,)), ((), ()))
    spec = lax.dot_general(fh[:, 0:MR], filt[...], nt, preferred_element_type=f32)
    spec = spec + lax.dot_general(fl[:, 0:MR], filt[...], nt, preferred_element_type=f32)
    hr, hi = spec[:HALF], spec[HALF:]
    top = lax.broadcasted_iota(jnp.int32, hr.shape, 0) == 0
    mid = jnp.where(top, 0.0, hi)
    low = jnp.where(top, hi, hr)

    for b in range(wins):
        start = win * b
        x = jnp.concatenate(
            [prod[0, start : start + NFFT, :], prod[1, start : start + NFFT, :]], axis=1
        ).astype(bf16)
        s = jnp.dot(fh[...], x, preferred_element_type=f32)
        sr, si = s[:HALF], s[HALF:]
        y = jnp.concatenate(
            [(hr * sr - mid * si).astype(bf16), (mid * sr + low * si).astype(bf16)], axis=0
        )
        medium = jnp.dot(g_mat[...], y, preferred_element_type=f32)[:win]
        first = FIRST + start
        gates = jnp.concatenate(
            [gate[0, first : first + win, :], gate[1, first : first + win, :]], axis=1
        )
        if begin == 0 and b == 0:
            head = halo[2 * HALO + 16 : 2 * HALO + 32, :].astype(f32)[16 - LEAD :]
            base = jnp.concatenate([head, stream[0 : win - LEAD, :].astype(f32)], axis=0)
        else:
            base = stream[begin + start - LEAD : begin + start - LEAD + win, :].astype(f32)
        value = base + gates * medium
        out[start : start + win, :] = value
        squared = value * value
        part = squared[:, :128] + squared[:, 128:]

        @pl.when(pl.program_id(0) == 0)
        def _():
            sq[start : start + win, :] = part

        @pl.when(pl.program_id(0) > 0)
        def _():
            sq[start : start + win, :] = sq[start : start + win, :] + part


def second_kernel(
    seg, count, lanes_count, whole, near, far, near_sq, far_sq, gain, taps, rates,
    prod, gate, states, gathered, nrm, held_total, send_sem, recv_sem,
    parts, sums, scale, sum_send, sum_recv, decay,
):
    n = seg * SEGS
    me = lax.axis_index("ctx")
    group = pl.program_id(0)
    groups = held_total.shape[0]

    def peer_copy(g, k):
        return pltpu.make_async_remote_copy(
            src_ref=held_total.at[g],
            dst_ref=gathered.at[g, me],
            send_sem=send_sem.at[g, k - 1],
            recv_sem=recv_sem.at[g, k - 1],
            device_id={"ctx": lax.rem(me + k, count)},
            device_id_type=pl.DeviceIdType.MESH,
        )

    @pl.when(group == 0)
    def _():
        barrier = pltpu.get_barrier_semaphore()

        def greet(k, c):
            pl.semaphore_signal(
                barrier, inc=1, device_id={"ctx": lax.rem(me + k, count)},
                device_id_type=pl.DeviceIdType.MESH,
            )
            return c

        lax.fori_loop(1, count, greet, 0)
        mine = lax.axis_index("tp")
        for k in range(1, lanes_count):
            pl.semaphore_signal(
                barrier, inc=1, device_id={"tp": lax.rem(mine + k, lanes_count)},
                device_id_type=pl.DeviceIdType.MESH,
            )
        pl.semaphore_wait(barrier, count - 1 + lanes_count - 1)

        half = near_sq.shape[0]
        scale[0:half, :] = near_sq[...]
        scale[half:n, :] = far_sq[...]
        scale[n:, :] = jnp.zeros((scale.shape[0] - n, 128), f32)
        parts[0] = lax.dot_general(
            jnp.ones((8, 128), f32), scale[...], (((1,), (1,)), ((), ())),
            precision=lax.Precision.HIGHEST, preferred_element_type=f32,
        )
        copies = [
            pltpu.make_async_remote_copy(
                src_ref=parts.at[0],
                dst_ref=parts.at[k],
                send_sem=sum_send.at[k - 1],
                recv_sem=sum_recv.at[k - 1],
                device_id={"tp": lax.rem(mine + k, lanes_count)},
                device_id_type=pl.DeviceIdType.MESH,
            )
            for k in range(1, lanes_count)
        ]
        for copy in copies:
            copy.start()
        for copy in copies:
            copy.wait()
        sums[...] = parts[0]
        for k in range(1, lanes_count):
            sums[...] = sums[...] + parts[k]
        column = lax.dot_general(
            sums[...], jnp.full((8, 128), 0.125, f32), (((0,), (0,)), ((), ())),
            precision=lax.Precision.HIGHEST, preferred_element_type=f32,
        )
        scale[...] = lax.rsqrt(column / whole + EPS)

    cut = near.shape[0]
    nrm[0:8, :] = jnp.zeros((8, 128), f32)
    nrm[8 : 8 + cut, :] = (near[...] * scale[0:cut, :] * gain[...]).astype(bf16).astype(f32)
    nrm[8 + cut : 8 + n, :] = (far[...] * scale[cut:n, :] * gain[...]).astype(bf16).astype(f32)
    place = lax.broadcasted_iota(jnp.int32, (SEGS, 128), 0) * seg
    left = ((SEGS - 1) * seg - place).astype(f32)
    decay[...] = jnp.exp(-rates[...])

    def step(t0, size, state):
        held = [nrm[pl.ds(t0 + j + 2, SEGS, stride=seg), :] for j in range(size + 6)]
        state = list(state)
        made = []
        for f in range(3):
            ws = [taps[f, k : k + 1, :] for k in range(TAPS)]
            made.append([tree([ws[k] * held[u + 6 - k] for k in range(TAPS)]) for u in range(size)])
        values = []
        for u in range(size):
            p = (made[1][u] * made[2][u]).astype(bf16).astype(f32)
            p = jnp.where(place + (t0 + u) >= LEAD, p, 0.0)
            prod[t0 + u] = p
            gate[t0 + u] = made[0][u]
            values.append(p)
        for m in range(MODES):
            d = decay[m : m + 1, :]
            for u in range(size):
                state[m] = state[m] * d + values[u]
        return tuple(state)

    zero = jnp.zeros((SEGS, 128), f32)
    state = steps(seg, 6, step, (zero,) * MODES)
    for m in range(MODES):
        states[m] = state[m]
        held_total[group, m : m + 1, :] = jnp.sum(
            state[m] * jnp.exp(-rates[m : m + 1, :] * left), axis=0, keepdims=True
        )

    def send(k, c):
        @pl.when(me + k < count)
        def _():
            peer_copy(group, k).start()

        return c

    lax.fori_loop(1, count, send, 0)

    @pl.when(group == groups - 1)
    def _():
        def finish(at, c):
            g, k = at // (count - 1), at % (count - 1) + 1

            @pl.when(me + k < count)
            def _():
                peer_copy(g, k).wait_send()

            @pl.when(me - k >= 0)
            def _():
                peer_copy(g, k).wait_recv()

            return c

        lax.fori_loop(0, groups * (count - 1), finish, 0)


def third_kernel(
    seg, count, prod, gate, states, totals, near, far, rates, weight, out, init, ybuf, decay
):
    n = seg * SEGS
    rows = n - LEAD
    me = lax.axis_index("ctx")
    r = rates[...]
    decay[...] = jnp.exp(-r)
    span = jnp.exp(-r * seg)
    row = jnp.zeros(r.shape, f32)
    for e in range(count):
        apart = jnp.full(r.shape, me - 1 - e, jnp.int32)
        coef = jnp.exp(-r * (jnp.maximum(apart, 0) * rows - LEAD).astype(f32))
        row = row + jnp.where(apart >= 0, coef * totals[0, e], 0.0)
    for s in range(SEGS):
        init[:, s, :] = row
        row = row * span + states[:, s, :]

    def step(t0, size, state):
        state = list(state)
        values = [prod[t0 + u] for u in range(size)]
        sums = [[None] * 2 for _ in range(size)]
        for m in range(MODES):
            d = decay[m : m + 1, :]
            w = weight[m : m + 1, :]
            for u in range(size):
                state[m] = state[m] * d + values[u]
                term = state[m] * w
                had = sums[u][m % 2]
                sums[u][m % 2] = term if had is None else had + term
        for u in range(size):
            ybuf[pl.ds(t0 + u, SEGS, stride=seg), :] = gate[t0 + u] * (sums[u][0] + sums[u][1])
        return tuple(state)

    steps(seg, 8, step, tuple(init[m] for m in range(MODES)))
    cut = near.shape[0]
    out[0 : cut - LEAD, :] = (near[LEAD:cut, :] + ybuf[LEAD:cut, :]).astype(bf16)
    out[cut - LEAD : n - LEAD, :] = (far[...] + ybuf[cut:n, :]).astype(bf16)


def params(**more):
    return pltpu.CompilerParams(
        dimension_semantics=("arbitrary",), vmem_limit_bytes=VMEM_LIMIT, **more
    )


def body(stream_in, features, mr_taps, mr_filter, norm_gain, li_taps, modal_rates, modal_weights):
    rows, _, width = features.shape
    count = lax.axis_size("ctx")
    whole = width * lax.axis_size("tp")
    ext = rows + LEAD
    feats = jnp.transpose(features, (1, 0, 2))
    taps_one = jnp.transpose(mr_taps, (0, 2, 1))
    taps_two = jnp.transpose(li_taps, (0, 2, 1))
    rates = jnp.transpose(modal_rates)
    weights = jnp.transpose(modal_weights)

    anywhere = pl.BlockSpec(memory_space=pl.ANY)
    tail = pl.pallas_call(
        functools.partial(tail_kernel, rows),
        in_specs=[anywhere, anywhere],
        out_specs=anywhere,
        out_shape=jax.ShapeDtypeStruct((2 * HALO + 32, width), bf16),
        scratch_shapes=[pltpu.SemaphoreType.DMA((4,))],
        compiler_params=pltpu.CompilerParams(vmem_limit_bytes=VMEM_LIMIT),
        name="tail",
    )(feats, stream_in)
    halo = lax.ppermute(tail, "ctx", [(i, i + 1) for i in range(count - 1)])

    wins = next(w for w in range(1, ext) if ext % w == 0 and (ext // w) % 8 == 0 and ext // w + FIRST <= NFFT)
    win = ext // wins
    padded = -(-win // 16) * 16
    (fh, fl), (gh, gl) = dft_tables(padded)
    cb = 256
    full = lambda shape: pl.BlockSpec(shape, lambda j: (0,) * len(shape))
    fh, fl, g_mat = jnp.asarray(fh), jnp.asarray(fl), jnp.asarray(gh)

    def medium(begin, count_wins, halo):
        out_rows = win * count_wins
        buf = max(HALO + rows - begin, (count_wins - 1) * win + NFFT)
        need = 512 if begin == 0 and rows % 512 == 0 else rows
        return pl.pallas_call(
            functools.partial(first_kernel, rows, win, count_wins, begin),
            grid=(width // cb,),
            in_specs=[
                pl.BlockSpec((3, need, cb), lambda j: (0, 0, j)),
                pl.BlockSpec((halo.shape[0], cb), lambda j: (0, j)),
                pl.BlockSpec((need, cb), lambda j: (0, j)),
                pl.BlockSpec((3, TAPS, cb), lambda j: (0, 0, j)),
                pl.BlockSpec((cb, MR), lambda j: (j, 0)),
                full((NFFT, NFFT)),
                full((NFFT, NFFT)),
                full((padded, NFFT)),
            ],
            out_specs=[
                pl.BlockSpec((out_rows, cb), lambda j: (0, j)),
                pl.BlockSpec((out_rows, 128), lambda j: (0, 0)),
            ],
            out_shape=[
                jax.ShapeDtypeStruct((out_rows, width), f32),
                jax.ShapeDtypeStruct((out_rows, 128), f32),
            ],
            scratch_shapes=[
                pltpu.VMEM((3, HALO + rows, 128), f32),
                pltpu.VMEM((2, buf, 128), f32),
                pltpu.VMEM((2, buf, 128), f32),
            ],
            compiler_params=params(),
            cost_estimate=pl.CostEstimate(
                flops=12_000_000_000 * count_wins, bytes_accessed=20_000_000 * count_wins, transcendentals=0
            ),
            name="medium_head" if begin == 0 else "medium_rest",
        )(feats, halo, stream_in, taps_one, mr_filter, fh, fl, g_mat)

    far, far_squares = medium(win, wins - 1, stream_in[:16])
    near, near_squares = medium(0, 1, halo)
    seg = ext // SEGS
    lanes_count = lax.axis_size("tp")
    scaled = weights * jnp.sqrt(-jnp.expm1(-2.0 * rates))
    summed = -(-ext // 128) * 128
    col = lambda *lead: pl.BlockSpec(lead + (128,), lambda j: (0,) * len(lead) + (j,))
    groups = width // 128
    prod, gate, states, totals = pl.pallas_call(
        functools.partial(second_kernel, seg, count, lanes_count, whole),
        grid=(width // 128,),
        in_specs=[
            col(win),
            col(ext - win),
            full((win, 128)),
            full((ext - win, 128)),
            col(1),
            col(3, TAPS),
            col(MODES),
        ],
        out_specs=[col(seg, SEGS), col(seg, SEGS), col(MODES, SEGS), pl.BlockSpec(memory_space=pl.ANY)],
        out_shape=[
            jax.ShapeDtypeStruct((seg, SEGS, width), f32),
            jax.ShapeDtypeStruct((seg, SEGS, width), f32),
            jax.ShapeDtypeStruct((MODES, SEGS, width), f32),
            jax.ShapeDtypeStruct((groups, count, MODES, 128), f32),
        ],
        scratch_shapes=[
            pltpu.VMEM((8 + ext, 128), f32),
            pltpu.VMEM((groups, MODES, 128), f32),
            pltpu.SemaphoreType.DMA((groups, count - 1)),
            pltpu.SemaphoreType.DMA((groups, count - 1)),
            pltpu.VMEM((lanes_count, 8, summed), f32),
            pltpu.VMEM((8, summed), f32),
            pltpu.VMEM((summed, 128), f32),
            pltpu.SemaphoreType.DMA((lanes_count - 1,)),
            pltpu.SemaphoreType.DMA((lanes_count - 1,)),
            pltpu.VMEM((MODES, 128), f32),
        ],
        compiler_params=params(collective_id=0, has_side_effects=True),
        name="states",
    )(near, far, near_squares, far_squares, norm_gain[None, :], taps_two, rates)

    return pl.pallas_call(
        functools.partial(third_kernel, seg, count),
        grid=(width // 128,),
        in_specs=[
            col(seg, SEGS),
            col(seg, SEGS),
            col(MODES, SEGS),
            pl.BlockSpec((1, count, MODES, 128), lambda j: (j, 0, 0, 0)),
            col(win),
            col(ext - win),
            col(MODES),
            col(MODES),
        ],
        out_specs=col(rows),
        out_shape=jax.ShapeDtypeStruct((rows, width), bf16),
        scratch_shapes=[pltpu.VMEM((MODES, SEGS, 128), f32), pltpu.VMEM((ext, 128), f32), pltpu.VMEM((MODES, 128), f32)],
        compiler_params=params(),
        name="mix",
    )(prod, gate, states, totals, near, far, rates, scaled)


def solution(mesh):
    in_specs = (
        P("ctx", "tp"),
        P("ctx", None, "tp"),
        P(None, "tp", None),
        P("tp", None),
        P("tp"),
        P(None, "tp", None),
        P("tp", None),
        P("tp", None),
    )
    return jax.shard_map(
        body, mesh=mesh, in_specs=in_specs, out_specs=P("ctx", "tp"), check_vma=False
    )
```

```python
import functools

import jax
import jax.numpy as jnp
import ml_dtypes
import numpy as np
from jax import lax
from jax.experimental import pallas as pl
from jax.experimental.pallas import tpu as pltpu
from jax.sharding import PartitionSpec as P

EPS = 1e-06
MODES = 16
TAPS = 7
MR = 128
HALO = 144
LEAD = 8
SEGS = 8
NFFT = 512
HALF = NFFT // 2
FIRST = HALO - LEAD
VMEM_LIMIT = 60 * 1024 * 1024
f32 = jnp.float32
bf16 = jnp.bfloat16


def split_np(matrix):
    high = matrix.astype(np.float32).astype(ml_dtypes.bfloat16)
    low = (matrix - high.astype(np.float64)).astype(np.float32).astype(ml_dtypes.bfloat16)
    return high, low


def dft_tables(out_rows):
    k = np.arange(HALF)[:, None]
    i = np.arange(NFFT)[None, :]
    angle = 2.0 * np.pi * ((k * i) % NFFT) / NFFT
    sign = 1.0 - 2.0 * (i % 2)
    forward = np.concatenate([np.cos(angle), -np.sin(angle)], axis=0)
    forward[HALF] = sign[0]
    back = 2.0 * forward.T / NFFT
    back[:, 0] *= 0.5
    back[:, HALF] *= 0.5
    return split_np(forward), split_np(back[FIRST : FIRST + out_rows])


def steps(count, unroll, step, carry):
    main = count // unroll
    carry = lax.fori_loop(0, main, lambda it, c: step(it * unroll, unroll, c), carry)
    if count % unroll:
        carry = step(main * unroll, count % unroll, carry)
    return carry


def tree(terms):
    while len(terms) > 1:
        terms = [sum(terms[i + 1 : i + 2], terms[i]) for i in range(0, len(terms), 2)]
    return terms[0]


def tail_kernel(rows, feats, stream, out, sems):
    copies = [
        pltpu.make_async_copy(source, out.at[place : place + size, :], sems.at[i])
        for i, (source, place, size) in enumerate(
            [
                (feats.at[1, rows - HALO : rows, :], 0, HALO),
                (feats.at[2, rows - HALO : rows, :], HALO, HALO),
                (feats.at[0, rows - 16 : rows, :], 2 * HALO, 16),
                (stream.at[rows - 16 : rows, :], 2 * HALO + 16, 16),
            ]
        )
    ]
    for copy in copies:
        copy.start()
    for copy in copies:
        copy.wait()


def first_kernel(
    rows, win, wins, begin, feat, halo, stream, taps, filt, fh, fl, g_mat, out, sq, xs, prod, gate
):
    low_row = 8 if begin == 0 else begin
    last = (begin // win + wins - 1) * win
    high = min(HALO + rows, last + FIRST + win if begin == 0 else HALO + rows)
    base_x = low_row - 8
    seg = (high - low_row) // SEGS
    tail = last + NFFT

    for g in range(2):
        lanes = slice(g * 128, g * 128 + 128)
        if begin == 0:
            own = high - HALO
            own16 = -(-own // 16) * 16
            for f in range(3):
                xs[f, HALO : HALO + own16, :] = feat[f, 0:own16, lanes].astype(f32)
            xs[0, HALO - 16 : HALO, :] = halo[2 * HALO : 2 * HALO + 16, lanes].astype(f32)
            xs[1, 0:HALO, :] = halo[0:HALO, lanes].astype(f32)
            xs[2, 0:HALO, :] = halo[HALO : 2 * HALO, lanes].astype(f32)
            shift = 0
        else:
            skip = (base_x - HALO) // 16 * 16
            shift = base_x - HALO - skip
            for f in range(3):
                xs[f, 0 : rows - skip, :] = feat[f, skip:rows, lanes].astype(f32)

        def step(t0, n, carry):
            made = []
            for f in range(3):
                held = [xs[f, pl.ds(t0 + j + 2 + shift, SEGS, stride=seg), :] for j in range(n + 6)]
                ws = [taps[f, k : k + 1, lanes] for k in range(TAPS)]
                made.append([tree([ws[k] * held[u + 6 - k] for k in range(TAPS)]) for u in range(n)])
            for u in range(n):
                at = pl.ds(t0 + u + low_row - begin, SEGS, stride=seg)
                prod[g, at, :] = made[1][u] * made[2][u]
                gate[g, at, :] = made[0][u]
            return carry

        steps(seg, 12, step, 0)
        if low_row > begin:
            prod[g, 0 : low_row - begin, :] = jnp.zeros((low_row - begin, 128), f32)
        if tail > high:
            prod[g, high - begin : tail - begin, :] = jnp.zeros((tail - high, 128), f32)

    nt = (((1,), (1,)), ((), ()))
    spec = lax.dot_general(fh[:, 0:MR], filt[...], nt, preferred_element_type=f32)
    spec = spec + lax.dot_general(fl[:, 0:MR], filt[...], nt, preferred_element_type=f32)
    hr, hi = spec[:HALF], spec[HALF:]
    top = lax.broadcasted_iota(jnp.int32, hr.shape, 0) == 0
    mid = jnp.where(top, 0.0, hi)
    low = jnp.where(top, hi, hr)

    for b in range(wins):
        start = win * b
        x = jnp.concatenate(
            [prod[0, start : start + NFFT, :], prod[1, start : start + NFFT, :]], axis=1
        ).astype(bf16)
        s = jnp.dot(fh[...], x, preferred_element_type=f32)
        sr, si = s[:HALF], s[HALF:]
        y = jnp.concatenate(
            [(hr * sr - mid * si).astype(bf16), (mid * sr + low * si).astype(bf16)], axis=0
        )
        medium = jnp.dot(g_mat[...], y, preferred_element_type=f32)[:win]
        first = FIRST + start
        gates = jnp.concatenate(
            [gate[0, first : first + win, :], gate[1, first : first + win, :]], axis=1
        )
        if begin == 0 and b == 0:
            head = halo[2 * HALO + 16 : 2 * HALO + 32, :].astype(f32)[16 - LEAD :]
            base = jnp.concatenate([head, stream[0 : win - LEAD, :].astype(f32)], axis=0)
        else:
            base = stream[begin + start - LEAD : begin + start - LEAD + win, :].astype(f32)
        value = base + gates * medium
        out[start : start + win, :] = value
        squared = value * value
        part = squared[:, :128] + squared[:, 128:]

        @pl.when(pl.program_id(0) == 0)
        def _():
            sq[start : start + win, :] = part

        @pl.when(pl.program_id(0) > 0)
        def _():
            sq[start : start + win, :] = sq[start : start + win, :] + part


def second_kernel(
    seg, count, lanes_count, whole, near, far, near_sq, far_sq, gain, taps, rates,
    prod, gate, states, gathered, nrm, held_total, send_sem, recv_sem,
    parts, sums, scale, sum_send, sum_recv, decay,
):
    n = seg * SEGS
    me = lax.axis_index("ctx")
    group = pl.program_id(0)
    groups = held_total.shape[0]

    def peer_copy(g, k):
        return pltpu.make_async_remote_copy(
            src_ref=held_total.at[g],
            dst_ref=gathered.at[g, me],
            send_sem=send_sem.at[g, k - 1],
            recv_sem=recv_sem.at[g, k - 1],
            device_id={"ctx": lax.rem(me + k, count)},
            device_id_type=pl.DeviceIdType.MESH,
        )

    @pl.when(group == 0)
    def _():
        barrier = pltpu.get_barrier_semaphore()

        def greet(k, c):
            pl.semaphore_signal(
                barrier, inc=1, device_id={"ctx": lax.rem(me + k, count)},
                device_id_type=pl.DeviceIdType.MESH,
            )
            return c

        lax.fori_loop(1, count, greet, 0)
        mine = lax.axis_index("tp")
        for k in range(1, lanes_count):
            pl.semaphore_signal(
                barrier, inc=1, device_id={"tp": lax.rem(mine + k, lanes_count)},
                device_id_type=pl.DeviceIdType.MESH,
            )
        pl.semaphore_wait(barrier, count - 1 + lanes_count - 1)

        half = near_sq.shape[0]
        scale[0:half, :] = near_sq[...]
        scale[half:n, :] = far_sq[...]
        scale[n:, :] = jnp.zeros((scale.shape[0] - n, 128), f32)
        parts[0] = lax.dot_general(
            jnp.ones((8, 128), f32), scale[...], (((1,), (1,)), ((), ())),
            precision=lax.Precision.HIGHEST, preferred_element_type=f32,
        )
        copies = [
            pltpu.make_async_remote_copy(
                src_ref=parts.at[0],
                dst_ref=parts.at[k],
                send_sem=sum_send.at[k - 1],
                recv_sem=sum_recv.at[k - 1],
                device_id={"tp": lax.rem(mine + k, lanes_count)},
                device_id_type=pl.DeviceIdType.MESH,
            )
            for k in range(1, lanes_count)
        ]
        for copy in copies:
            copy.start()
        for copy in copies:
            copy.wait()
        sums[...] = parts[0]
        for k in range(1, lanes_count):
            sums[...] = sums[...] + parts[k]
        column = lax.dot_general(
            sums[...], jnp.full((8, 128), 0.125, f32), (((0,), (0,)), ((), ())),
            precision=lax.Precision.HIGHEST, preferred_element_type=f32,
        )
        scale[...] = lax.rsqrt(column / whole + EPS)

    cut = near.shape[0]
    nrm[0:8, :] = jnp.zeros((8, 128), f32)
    nrm[8 : 8 + cut, :] = (near[...] * scale[0:cut, :] * gain[...]).astype(bf16).astype(f32)
    nrm[8 + cut : 8 + n, :] = (far[...] * scale[cut:n, :] * gain[...]).astype(bf16).astype(f32)
    place = lax.broadcasted_iota(jnp.int32, (SEGS, 128), 0) * seg
    left = ((SEGS - 1) * seg - place).astype(f32)
    decay[...] = jnp.exp(-rates[...])

    def step(t0, size, state):
        held = [nrm[pl.ds(t0 + j + 2, SEGS, stride=seg), :] for j in range(size + 6)]
        state = list(state)
        made = []
        for f in range(3):
            ws = [taps[f, k : k + 1, :] for k in range(TAPS)]
            made.append([tree([ws[k] * held[u + 6 - k] for k in range(TAPS)]) for u in range(size)])
        values = []
        for u in range(size):
            p = (made[1][u] * made[2][u]).astype(bf16).astype(f32)
            p = jnp.where(place + (t0 + u) >= LEAD, p, 0.0)
            prod[t0 + u] = p
            gate[t0 + u] = made[0][u]
            values.append(p)
        for m in range(MODES):
            d = decay[m : m + 1, :]
            for u in range(size):
                state[m] = state[m] * d + values[u]
        return tuple(state)

    zero = jnp.zeros((SEGS, 128), f32)
    state = steps(seg, 6, step, (zero,) * MODES)
    for m in range(MODES):
        states[m] = state[m]
        held_total[group, m : m + 1, :] = jnp.sum(
            state[m] * jnp.exp(-rates[m : m + 1, :] * left), axis=0, keepdims=True
        )

    def send(k, c):
        @pl.when(me + k < count)
        def _():
            peer_copy(group, k).start()

        return c

    lax.fori_loop(1, count, send, 0)

    @pl.when(group == groups - 1)
    def _():
        def finish(at, c):
            g, k = at // (count - 1), at % (count - 1) + 1

            @pl.when(me + k < count)
            def _():
                peer_copy(g, k).wait_send()

            @pl.when(me - k >= 0)
            def _():
                peer_copy(g, k).wait_recv()

            return c

        lax.fori_loop(0, groups * (count - 1), finish, 0)


def third_kernel(
    seg, count, prod, gate, states, totals, near, far, rates, weight, out, init, ybuf, decay
):
    n = seg * SEGS
    rows = n - LEAD
    me = lax.axis_index("ctx")
    r = rates[...]
    decay[...] = jnp.exp(-r)
    span = jnp.exp(-r * seg)
    row = jnp.zeros(r.shape, f32)
    for e in range(count):
        apart = jnp.full(r.shape, me - 1 - e, jnp.int32)
        coef = jnp.exp(-r * (jnp.maximum(apart, 0) * rows - LEAD).astype(f32))
        row = row + jnp.where(apart >= 0, coef * totals[0, e], 0.0)
    for s in range(SEGS):
        init[:, s, :] = row
        row = row * span + states[:, s, :]

    def step(t0, size, state):
        state = list(state)
        values = [prod[t0 + u] for u in range(size)]
        sums = [[None] * 2 for _ in range(size)]
        for m in range(MODES):
            d = decay[m : m + 1, :]
            w = weight[m : m + 1, :]
            for u in range(size):
                state[m] = state[m] * d + values[u]
                term = state[m] * w
                had = sums[u][m % 2]
                sums[u][m % 2] = term if had is None else had + term
        for u in range(size):
            ybuf[pl.ds(t0 + u, SEGS, stride=seg), :] = gate[t0 + u] * (sums[u][0] + sums[u][1])
        return tuple(state)

    steps(seg, 8, step, tuple(init[m] for m in range(MODES)))
    cut = near.shape[0]
    out[0 : cut - LEAD, :] = (near[LEAD:cut, :] + ybuf[LEAD:cut, :]).astype(bf16)
    out[cut - LEAD : n - LEAD, :] = (far[...] + ybuf[cut:n, :]).astype(bf16)


def params(**more):
    return pltpu.CompilerParams(
        dimension_semantics=("arbitrary",), vmem_limit_bytes=VMEM_LIMIT, **more
    )


def body(stream_in, features, mr_taps, mr_filter, norm_gain, li_taps, modal_rates, modal_weights):
    rows, _, width = features.shape
    count = lax.axis_size("ctx")
    whole = width * lax.axis_size("tp")
    ext = rows + LEAD
    feats = jnp.transpose(features, (1, 0, 2))
    taps_one = jnp.transpose(mr_taps, (0, 2, 1))
    taps_two = jnp.transpose(li_taps, (0, 2, 1))
    rates = jnp.transpose(modal_rates)
    weights = jnp.transpose(modal_weights)

    anywhere = pl.BlockSpec(memory_space=pl.ANY)
    tail = pl.pallas_call(
        functools.partial(tail_kernel, rows),
        in_specs=[anywhere, anywhere],
        out_specs=pl.BlockSpec(memory_space=pltpu.VMEM),
        out_shape=jax.ShapeDtypeStruct((2 * HALO + 32, width), bf16),
        scratch_shapes=[pltpu.SemaphoreType.DMA((4,))],
        compiler_params=pltpu.CompilerParams(vmem_limit_bytes=VMEM_LIMIT),
        name="tail",
    )(feats, stream_in)
    halo = lax.ppermute(tail, "ctx", [(i, i + 1) for i in range(count - 1)])

    wins = next(w for w in range(1, ext) if ext % w == 0 and (ext // w) % 8 == 0 and ext // w + FIRST <= NFFT)
    win = ext // wins
    padded = -(-win // 16) * 16
    (fh, fl), (gh, gl) = dft_tables(padded)
    cb = 256
    full = lambda shape: pl.BlockSpec(shape, lambda j: (0,) * len(shape))
    fh, fl, g_mat = jnp.asarray(fh), jnp.asarray(fl), jnp.asarray(gh)

    def medium(begin, count_wins, halo):
        out_rows = win * count_wins
        buf = max(HALO + rows - begin, (count_wins - 1) * win + NFFT)
        need = 512 if begin == 0 and rows % 512 == 0 else rows
        return pl.pallas_call(
            functools.partial(first_kernel, rows, win, count_wins, begin),
            grid=(width // cb,),
            in_specs=[
                pl.BlockSpec((3, need, cb), lambda j: (0, 0, j)),
                pl.BlockSpec((halo.shape[0] if begin == 0 else 16, cb), lambda j: (0, j)),
                pl.BlockSpec((need, cb), lambda j: (0, j)),
                pl.BlockSpec((3, TAPS, cb), lambda j: (0, 0, j)),
                pl.BlockSpec((cb, MR), lambda j: (j, 0)),
                full((NFFT, NFFT)),
                full((NFFT, NFFT)),
                full((padded, NFFT)),
            ],
            out_specs=[
                pl.BlockSpec((out_rows, cb), lambda j: (0, j)),
                pl.BlockSpec((out_rows, 128), lambda j: (0, 0)),
            ],
            out_shape=[
                jax.ShapeDtypeStruct((out_rows, width), f32),
                jax.ShapeDtypeStruct((out_rows, 128), f32),
            ],
            scratch_shapes=[
                pltpu.VMEM((3, HALO + rows, 128), f32),
                pltpu.VMEM((2, buf, 128), f32),
                pltpu.VMEM((2, buf, 128), f32),
            ],
            compiler_params=params(),
            cost_estimate=pl.CostEstimate(
                flops=12_000_000_000 * count_wins, bytes_accessed=20_000_000 * count_wins, transcendentals=0
            ),
            name="medium_head" if begin == 0 else "medium_rest",
        )(feats, halo, stream_in, taps_one, mr_filter, fh, fl, g_mat)

    far, far_squares = medium(win, wins - 1, stream_in)
    near, near_squares = medium(0, 1, halo)
    seg = ext // SEGS
    lanes_count = lax.axis_size("tp")
    scaled = weights * jnp.sqrt(-jnp.expm1(-2.0 * rates))
    summed = -(-ext // 128) * 128
    col = lambda *lead: pl.BlockSpec(lead + (128,), lambda j: (0,) * len(lead) + (j,))
    groups = width // 128
    prod, gate, states, totals = pl.pallas_call(
        functools.partial(second_kernel, seg, count, lanes_count, whole),
        grid=(width // 128,),
        in_specs=[
            col(win),
            col(ext - win),
            full((win, 128)),
            full((ext - win, 128)),
            col(1),
            col(3, TAPS),
            col(MODES),
        ],
        out_specs=[col(seg, SEGS), col(seg, SEGS), col(MODES, SEGS), pl.BlockSpec(memory_space=pl.ANY)],
        out_shape=[
            jax.ShapeDtypeStruct((seg, SEGS, width), f32),
            jax.ShapeDtypeStruct((seg, SEGS, width), f32),
            jax.ShapeDtypeStruct((MODES, SEGS, width), f32),
            jax.ShapeDtypeStruct((groups, count, MODES, 128), f32),
        ],
        scratch_shapes=[
            pltpu.VMEM((8 + ext, 128), f32),
            pltpu.VMEM((groups, MODES, 128), f32),
            pltpu.SemaphoreType.DMA((groups, count - 1)),
            pltpu.SemaphoreType.DMA((groups, count - 1)),
            pltpu.VMEM((lanes_count, 8, summed), f32),
            pltpu.VMEM((8, summed), f32),
            pltpu.VMEM((summed, 128), f32),
            pltpu.SemaphoreType.DMA((lanes_count - 1,)),
            pltpu.SemaphoreType.DMA((lanes_count - 1,)),
            pltpu.VMEM((MODES, 128), f32),
        ],
        compiler_params=params(collective_id=0, has_side_effects=True),
        name="states",
    )(near, far, near_squares, far_squares, norm_gain[None, :], taps_two, rates)

    return pl.pallas_call(
        functools.partial(third_kernel, seg, count),
        grid=(width // 128,),
        in_specs=[
            col(seg, SEGS),
            col(seg, SEGS),
            col(MODES, SEGS),
            pl.BlockSpec((1, count, MODES, 128), lambda j: (j, 0, 0, 0)),
            col(win),
            col(ext - win),
            col(MODES),
            col(MODES),
        ],
        out_specs=col(rows),
        out_shape=jax.ShapeDtypeStruct((rows, width), bf16),
        scratch_shapes=[pltpu.VMEM((MODES, SEGS, 128), f32), pltpu.VMEM((ext, 128), f32), pltpu.VMEM((MODES, 128), f32)],
        compiler_params=params(),
        name="mix",
    )(prod, gate, states, totals, near, far, rates, scaled)


def solution(mesh):
    in_specs = (
        P("ctx", "tp"),
        P("ctx", None, "tp"),
        P(None, "tp", None),
        P("tp", None),
        P("tp"),
        P(None, "tp", None),
        P("tp", None),
        P("tp", None),
    )
    return jax.shard_map(
        body, mesh=mesh, in_specs=in_specs, out_specs=P("ctx", "tp"), check_vma=False
    )
```
